32 devices in a mesh: sky: 4 (over z), tile: 8 (over y, x, core).
Axes of the slice: x: 2, y: 2, z: 4, core: 2. Of those that a mesh axis runs over, the one named last changes fastest.
Arguments:
- science: float32 [4, 8, 2, 128, 512], P('sky', 'tile'), may hold values from -6 to 6
- inverse_variance: bfloat16 [4, 8, 2, 128, 512], P('sky', 'tile'), may hold values from 0.25 to 4
- template: bfloat16 [4, 8, 128, 512], P('sky', 'tile'), may hold values from -6 to 6
- filters: bfloat16 [8, 21], replicated, may hold values from -1.25 to 1.25
- kernel_index: int32 [20, 2], replicated, may hold values from 0 to 7
- spatial_coeff: float32 [4, 8, 2, 3, 20], P('sky', 'tile'), may hold values from -1.5 to 1.5
- visit_offset: int32 [4, 2], P('sky'), may hold values from 0 to 7
- block_count: int32 [4, 8, 2], P('sky', 'tile'), may hold values from 12 to 16, as said below
- block_owner: int32 [4, 8, 32], P('sky', 'tile'), may hold values from 0 to 7, as said below
- block_slot: int32 [4, 8, 32], P('sky', 'tile'), may hold values from 0 to 2
- coadd_sum: float32 [4, 8, 3, 4096], P('sky', 'tile'), may hold values from -18 to 18
- coadd_weight: float32 [4, 8, 3, 4096], P('sky', 'tile'), may hold values from 2 to 8
Outputs:
- difference: float32 [4, 8, 2, 128, 512], P('sky', 'tile')
- coadd: float32 [4, 8, 3, 4096], P('sky', 'tile')
The draws below stay inside these ranges and needn't reach their ends.
Inputs may be any that keep to these rules, and one draw needn't show every extreme that they name: `visit_offset`: exposure tile i of a group lies in visit v on template tile (i + offset) mod 8. `block_count`: blocks 0 to count - 1 of a tile and visit enter the coadd. `block_owner`: among the 32 blocks of one device no owner appears more than 6 times; in each sky group one owner receives exactly 6 blocks from every device of the group, their first 6 blocks.
All inputs are finite; a program needn't handle non-finite values.
Results may differ from the reference program's by a relative error of at most 0.0026.
Values may be sent and summed in bfloat16 or wider, within the bound.
A program may use at most 64 MiB of HBM per device.

```python
import math
import jax
import jax.numpy as jnp
from jax import lax

H = 128
W = 512
VISITS = 2
NBASIS = 8
KERNELS = 20
TAPS = 21
HALF = 10
BS = 64
PATCH_DEV = 3
GROUPS = 4
TILES = 8
BPV = 16
NBLK = 32
CAP = 6


def draw_block_count(key, part):
    entry_total = GROUPS * TILES * VISITS
    lowered = jax.random.randint(jax.random.fold_in(key, 11), (entry_total,), 0, BPV // 4 + 1)
    counts = BPV - lowered
    chosen_spot = jax.random.randint(jax.random.fold_in(key, 12), (), 0, entry_total)
    position = jnp.arange(entry_total, dtype=jnp.int32)
    counts = jnp.where(position == chosen_spot, BPV, counts)
    counts = jnp.where(position == (chosen_spot + 1) % entry_total, BPV - BPV // 4, counts)
    return counts.reshape(GROUPS, TILES, VISITS).astype(jnp.int32)


def draw_block_owner(key, part):
    hot_owner = jax.random.randint(jax.random.fold_in(key, 21), (GROUPS, 1, 1), 0, TILES)
    pool_size = TILES * CAP
    base_owner = jnp.arange(pool_size, dtype=jnp.int32) % TILES
    device_keys = jax.random.split(jax.random.fold_in(key, 22), GROUPS * TILES)
    shuffled = jax.vmap(lambda k: jax.random.permutation(k, pool_size))(device_keys)
    owners = base_owner[shuffled].reshape(GROUPS, TILES, pool_size)
    position = jnp.arange(pool_size, dtype=jnp.int32)[None, None, :]
    score = jnp.where(owners == hot_owner, position - pool_size, position)
    ordering = jnp.argsort(score, axis=-1, stable=True)
    ordered = jnp.take_along_axis(owners, ordering, axis=-1)
    return ordered[..., :NBLK].astype(jnp.int32)


def plant(drawn, rng, smallest, largest):
    extent = drawn.shape
    place = [jax.random.randint(jax.random.fold_in(rng, axis), (), 0, extent[axis]) for axis in range(len(extent))]
    drawn = drawn.at[tuple(place)].set(smallest)
    longest = extent.index(max(extent))
    place[longest] = (place[longest] + 1) % extent[longest]
    return drawn.at[tuple(place)].set(largest)


def block_levels(stream_key, shape, shards, smallest, high):
    def one(dim, parts):
        draws = jax.random.uniform(jax.random.fold_in(jax.random.fold_in(stream_key, 6), dim), (parts,), jnp.float32, smallest / len(shards), high / len(shards))
        return jnp.repeat(jnp.exp(draws), shape[dim] // parts).reshape((-1,) + (1,) * (len(shape) - dim - 1))

    level = one(*shards[0])
    for cut in shards[1:]:
        level = level * one(*cut)
    return level


def scatter_about(stream_key, dims, spread, bound, cuts=(), kind=jnp.bfloat16):
    array = spread * jax.random.normal(stream_key, dims, jnp.float32)
    if cuts:
        array = array * block_levels(stream_key, dims, cuts, -0.22, 0.18)
    return jnp.clip(array, -bound, bound).astype(kind)


def setup_inputs(seed: int = 0) -> dict:
    key_of = jax.random.split(jax.random.key(seed), 13)
    return {
        "science": scatter_about(key_of[0], (GROUPS, TILES, VISITS, H, W), 1.0, 6.0, ((0, 4), (1, 8)), jnp.float32),
        "inverse_variance": jnp.clip(jnp.exp(math.log(4.0) - 2.7725887 * jax.random.uniform(key_of[1], (GROUPS, TILES, VISITS, H, W), jnp.float32) ** block_levels(key_of[1], (GROUPS, TILES, VISITS, H, W), ((0, 4), (1, 8)), -0.2, 0.2)), 0.25, 4.0).astype(jnp.bfloat16),
        "template": scatter_about(key_of[2], (GROUPS, TILES, H, W), 1.0, 6.0, ((0, 4), (1, 8))),
        "filters": scatter_about(key_of[3], (NBASIS, TAPS), TAPS ** -0.5, 1.25),
        "kernel_index": plant(jax.random.randint(key_of[4], (KERNELS, 2), 0, NBASIS), jax.random.fold_in(key_of[4], 1), 0, NBASIS - 1).astype(jnp.int32),
        "spatial_coeff": scatter_about(key_of[5], (GROUPS, TILES, VISITS, 3, KERNELS), 0.25, 1.5, ((0, 4), (1, 8)), jnp.float32),
        "visit_offset": plant(jax.random.randint(key_of[6], (GROUPS, VISITS), 0, TILES), jax.random.fold_in(key_of[6], 1), 0, TILES - 1).astype(jnp.int32),
        "block_count": draw_block_count(jax.random.fold_in(key_of[12], 71), 0),
        "block_owner": draw_block_owner(jax.random.fold_in(key_of[12], 71), 0),
        "block_slot": plant(jax.random.randint(key_of[9], (GROUPS, TILES, NBLK), 0, PATCH_DEV), jax.random.fold_in(key_of[9], 1), 0, PATCH_DEV - 1).astype(jnp.int32),
        "coadd_sum": scatter_about(key_of[10], (GROUPS, TILES, PATCH_DEV, BS * BS), 3.0, 18.0, ((0, 4), (1, 8)), jnp.float32),
        "coadd_weight": jnp.clip(jnp.exp(math.log(8.0) - 1.3862944 * jax.random.uniform(key_of[11], (GROUPS, TILES, PATCH_DEV, BS * BS), jnp.float32) ** block_levels(key_of[11], (GROUPS, TILES, PATCH_DEV, BS * BS), ((0, 4), (1, 8)), -0.2, 0.2)), 2.0, 8.0),
    }


def block_rows(image):
    leading = image.shape[:-3]
    lead_count = len(leading)
    pieces = image.reshape(leading + (VISITS, H // BS, BS, W // BS, BS))
    axis_order = tuple(range(lead_count)) + (lead_count, lead_count + 1, lead_count + 3, lead_count + 2, lead_count + 4)
    return jnp.transpose(pieces, axis_order).reshape(leading + (NBLK, BS * BS))


def group_update(inputs, filter_taps, kernel_index):
    science, inverse_variance, template, spatial_coeff, visit_offset, block_count, block_owner, block_slot = inputs
    tile_ids = (jnp.arange(TILES, dtype=jnp.int32)[None, :] + visit_offset[:, None]) % TILES
    aligned = jnp.transpose(template[tile_ids], (1, 0, 2, 3))
    padded = jnp.pad(aligned, ((0, 0), (0, 0), (0, 0), (HALF, HALF)))

    def row_filter(row_taps):
        running = jnp.zeros(aligned.shape, jnp.float32)
        for q in range(TAPS):
            running = running + row_taps[q] * padded[..., q:q + W].astype(jnp.float32)
        return running.astype(jnp.bfloat16)

    filtered = lax.map(row_filter, filter_taps)
    across = (2.0 * jnp.arange(W, dtype=jnp.float32) + 1.0 - W) / W
    downward = (2.0 * jnp.arange(H, dtype=jnp.float32) + 1.0 - H) / H

    def add_kernel(matched, kernel_item):
        index_pair, kernel_coeff = kernel_item
        source = filtered[index_pair[0]]
        column_taps = filter_taps[index_pair[1]]
        shifted = jnp.pad(source, ((0, 0), (0, 0), (HALF, HALF), (0, 0)))
        convolved = jnp.zeros(source.shape, jnp.float32)
        for p in range(TAPS):
            convolved = convolved + column_taps[p] * shifted[:, :, p:p + H, :].astype(jnp.float32)
        weight_map = kernel_coeff[..., 0, None, None] + kernel_coeff[..., 1, None, None] * across + kernel_coeff[..., 2, None, None] * downward[:, None]
        return matched + weight_map * convolved, None

    matched, unused = lax.scan(add_kernel, jnp.zeros(aligned.shape, jnp.float32), (kernel_index, jnp.moveaxis(spatial_coeff, -1, 0)))
    difference = science - matched
    inverse = inverse_variance.astype(jnp.float32)
    weighted = block_rows(inverse * difference)
    weight_rows = block_rows(inverse)
    row_index = jnp.arange(NBLK, dtype=jnp.int32)
    is_valid = (row_index % BPV)[None, :] < jnp.repeat(block_count, BPV, axis=1)
    row_mask = is_valid.astype(jnp.float32)[..., None]
    destination = (block_owner * PATCH_DEV + block_slot).reshape(-1)
    sums = jax.ops.segment_sum((weighted * row_mask).reshape(-1, BS * BS), destination, num_segments=TILES * PATCH_DEV)
    weights = jax.ops.segment_sum((weight_rows * row_mask).reshape(-1, BS * BS), destination, num_segments=TILES * PATCH_DEV)
    return difference, sums.reshape(TILES, PATCH_DEV, BS * BS), weights.reshape(TILES, PATCH_DEV, BS * BS)


def share_edges(totals):
    lower = jnp.concatenate([jnp.zeros_like(totals[:1, :, -1]), totals[:-1, :, -1]], axis=0)
    upper = jnp.concatenate([totals[1:, :, 0], jnp.zeros_like(totals[:1, :, 0])], axis=0)
    return totals.at[:, :, 0].add(lower).at[:, :, -1].add(upper)


def reference(science, inverse_variance, template, filters, kernel_index, spatial_coeff, visit_offset, block_count, block_owner, block_slot, coadd_sum, coadd_weight):
    filter_taps = filters.astype(jnp.float32)

    def one_group(inputs):
        return group_update(inputs, filter_taps, kernel_index)

    difference, sums, weights = lax.map(one_group, (science, inverse_variance, template, spatial_coeff, visit_offset, block_count, block_owner, block_slot))
    merged_sums = share_edges(sums)
    merged_weights = share_edges(weights)
    coadd = (coadd_sum + merged_sums) / (coadd_weight + merged_weights)
    return difference, coadd
```

```python
import functools

import jax
import jax.numpy as jnp
from jax import lax
from jax.experimental import pallas as pl
from jax.experimental.pallas import tpu as pltpu
from jax.sharding import PartitionSpec as P

BS = 64
LANES = 128
MESH = pl.DeviceIdType.MESH
F32 = jnp.float32
BF16 = jnp.bfloat16


def greet(peers):
    barrier = pltpu.get_barrier_semaphore()
    for peer in peers:
        pl.semaphore_signal(barrier, inc=1, device_id=peer, device_id_type=MESH)
    return barrier


def align_kernel(n, visits, offset_ref, template_ref, out_ref, own, held, outgoing, send1, recv1, send2, recv2):
    sky = lax.axis_index("sky")
    me = lax.axis_index("tile")
    peers = [lax.rem(me + k, n) for k in range(1, n)]
    barrier = greet([(sky, peer) for peer in peers])
    height, width = template_ref.shape[-2:]
    tiles = width // LANES
    strip = height * tiles // n
    for t in range(tiles):
        own[t * height : (t + 1) * height, :] = template_ref[0, 0, :, t * LANES : (t + 1) * LANES]
    pl.semaphore_wait(barrier, n - 1)
    first = []
    for k, peer in enumerate(peers):
        copy = pltpu.make_async_remote_copy(
            src_ref=own.at[pl.ds(pl.multiple_of(peer * strip, strip), strip)],
            dst_ref=held.at[me],
            send_sem=send1.at[k],
            recv_sem=recv1.at[k],
            device_id=(sky, peer),
            device_id_type=MESH,
        )
        copy.start()
        first.append(copy)
    held[me] = own[pl.ds(pl.multiple_of(me * strip, strip), strip), :]
    for copy in first:
        copy.wait_recv()
    second = []
    for k, peer in enumerate(peers):
        for v in range(visits):
            place = peer + offset_ref[0, v]
            place = jnp.where(place >= n, place - n, place)
            outgoing[k, v] = held[place]
        copy = pltpu.make_async_remote_copy(
            src_ref=outgoing.at[k],
            dst_ref=out_ref.at[me],
            send_sem=send2.at[k],
            recv_sem=recv2.at[k],
            device_id=(sky, peer),
            device_id_type=MESH,
        )
        copy.start()
        second.append(copy)
    for v in range(visits):
        place = me + offset_ref[0, v]
        place = jnp.where(place >= n, place - n, place)
        out_ref[me, v] = held[place]
    for copy in first:
        copy.wait_send()
    for copy in second:
        copy.wait()


def toeplitz(rows):
    return pltpu.roll(rows, 0, 1, stride=1, stride_axis=0)


def match_kernel(
    patch_total,
    patches,
    strips_ref,
    filters_ref,
    index_ref,
    coeff_ref,
    science_ref,
    inverse_ref,
    count_ref,
    owner_ref,
    slot_ref,
    diff_ref,
    pay_ref,
    filtered,
    row_band,
    band_high,
    band_low,
    image,
    total,
):
    n, visits, strip, lanes = strips_ref.shape
    height, width = science_ref.shape[-2:]
    tiles = width // LANES
    basis, taps = filters_ref.shape
    half = taps // 2
    kernels = index_ref.shape[0]

    tap_id = lax.broadcasted_iota(jnp.int32, (taps, LANES), 0)
    lane_id = lax.broadcasted_iota(jnp.int32, (taps, LANES), 1)
    spread_row = (lane_id == lax.rem(half - tap_id + LANES, LANES)).astype(BF16)
    spread_col = (lane_id == lax.rem(tap_id - half + LANES, LANES)).astype(BF16)
    filters = filters_ref[...]
    row_taps = jnp.dot(filters, spread_row, preferred_element_type=F32)
    col_taps = jnp.dot(filters, spread_col, preferred_element_type=F32).astype(BF16)

    y = lax.broadcasted_iota(jnp.int32, (height, LANES), 0)
    x = lax.broadcasted_iota(jnp.int32, (height, LANES), 1)
    gap = y - x
    near = jnp.abs(gap) <= half
    before = gap >= LANES - half
    after = gap <= half - LANES
    for j in range(basis):
        full = toeplitz(jnp.broadcast_to(row_taps[j : j + 1, :], (LANES, LANES)))
        span = slice(j * LANES, (j + 1) * LANES)
        row_band[0:LANES, span] = jnp.where(before, full, 0.0).astype(BF16)
        row_band[LANES : 2 * LANES, span] = jnp.where(near, full, 0.0).astype(BF16)
        row_band[2 * LANES : 3 * LANES, span] = jnp.where(after, full, 0.0).astype(BF16)

    index = index_ref[...]
    basis_id = lax.broadcasted_iota(jnp.int32, (kernels, basis), 1)
    pick_col = (index[:, 1:2] == basis_id).astype(BF16)
    kernel_taps = jnp.dot(pick_col, col_taps, preferred_element_type=F32)
    spread = jnp.concatenate(
        [jnp.where(index[:, 0:1] == j, kernel_taps, 0.0) for j in range(basis)], axis=1
    )
    downward = (2.0 * y.astype(F32) + (1.0 - height)) / height
    for v in range(visits):
        mixed = jnp.dot(
            coeff_ref[0, 0, v], spread, precision=lax.Precision.HIGHEST, preferred_element_type=F32
        )
        for j in range(basis):
            span = slice(j * LANES, (j + 1) * LANES)
            steady = mixed[0:1, span] + downward * mixed[2:3, span]
            across = jnp.broadcast_to(mixed[1:2, span], (height, LANES))
            for part, rows in enumerate((steady, across)):
                band = jnp.where(near, toeplitz(rows), 0.0)
                high = band.astype(BF16)
                down = slice(part * height, (part + 1) * height)
                band_high[v, down, span] = high
                band_low[v, down, span] = (band - high.astype(F32)).astype(BF16)

    per_tile = height // strip if strip <= height else 1
    source = []
    for t in range(tiles):
        rows = []
        for v in range(visits):
            rows += [strips_ref[t * per_tile + s, v] for s in range(per_tile)]
        source.append(jnp.concatenate(rows, axis=0))
    for t in range(tiles):
        low, top = max(t - 1, 0), min(t + 2, tiles)
        window = jnp.concatenate(source[low:top], axis=1)
        band = row_band[(low - t + 1) * LANES : (top - t + 1) * LANES, :]
        out = jnp.dot(window, band, preferred_element_type=F32).astype(BF16)
        for v in range(visits):
            for j in range(basis):
                filtered[v, j * height : (j + 1) * height, t * LANES : (t + 1) * LANES] = out[
                    v * height : (v + 1) * height, j * LANES : (j + 1) * LANES
                ]

    total[...] = jnp.zeros_like(total)
    x_id = lax.broadcasted_iota(jnp.int32, (1, width), 1).astype(F32)
    rightward = (2.0 * x_id + (1.0 - width)) / width
    low_lanes = lax.broadcasted_iota(jnp.int32, (BS // 2, LANES), 1) < BS
    downs = height // BS
    blocks = downs * (width // BS)
    for v in range(visits):
        operand = filtered[v]
        product = jnp.dot(band_high[v], operand, preferred_element_type=F32) + jnp.dot(
            band_low[v], operand, preferred_element_type=F32
        )
        difference = science_ref[0, 0, v] - (product[:height] + rightward * product[height:])
        diff_ref[0, 0, v] = difference
        inverse = inverse_ref[0, 0, v].astype(F32)
        weighted = inverse * difference
        for t in range(tiles):
            image[0, t] = weighted[:, t * LANES : (t + 1) * LANES]
            image[1, t] = inverse[:, t * LANES : (t + 1) * LANES]
        limit = count_ref[0, 0, v]
        for by in range(downs):
            for t in range(tiles):
                pair = []
                for side in range(2):
                    r = by * (width // BS) + 2 * t + side
                    spot = owner_ref[0, 0, v * blocks + r] * patches + slot_ref[0, 0, v * blocks + r]
                    pair.append(jnp.where(r < limit, spot, patch_total))
                for m in range(2):
                    even = image[m, t, pl.ds(by * BS, BS // 2, stride=2), :]
                    odd = image[m, t, pl.ds(by * BS + 1, BS // 2, stride=2), :]
                    left = jnp.where(low_lanes, even, pltpu.roll(odd, BS, 1))
                    right = jnp.where(low_lanes, pltpu.roll(even, BS, 1), odd)
                    total[pair[0], m] += left
                    total[pair[1], m] += right
    pay_ref[...] = total[0:patch_total].astype(BF16)


def merge_kernel(
    n, skies, patches, pay_ref, sum_ref, weight_ref, out_ref, landed, merged, edge, halo, send, recv, edge_send, edge_recv
):
    sky = lax.axis_index("sky")
    me = lax.axis_index("tile")
    peers = [lax.rem(me + k, n) for k in range(1, n)]
    barrier = greet([(sky, peer) for peer in peers])
    has_low = sky > 0
    has_high = sky < skies - 1

    @pl.when(has_low)
    def _():
        pl.semaphore_signal(barrier, inc=1, device_id=(sky - 1, me), device_id_type=MESH)

    @pl.when(has_high)
    def _():
        pl.semaphore_signal(barrier, inc=1, device_id=(sky + 1, me), device_id_type=MESH)

    around = jnp.where(has_low, 1, 0) + jnp.where(has_high, 1, 0)
    pl.semaphore_wait(barrier, n - 1 + around)
    copies = []
    for k, peer in enumerate(peers):
        copy = pltpu.make_async_remote_copy(
            src_ref=pay_ref.at[pl.ds(peer * patches, patches)],
            dst_ref=landed.at[k],
            send_sem=send.at[k],
            recv_sem=recv.at[k],
            device_id=(sky, peer),
            device_id_type=MESH,
        )
        copy.start()
        copies.append(copy)
    summed = pay_ref[pl.ds(me * patches, patches)].astype(F32)
    for k, copy in enumerate(copies):
        copy.wait_recv()
        summed = summed + landed[k].astype(F32)
    merged[...] = summed
    edge[0] = summed[0].astype(BF16)
    edge[1] = summed[patches - 1].astype(BF16)
    to_low = pltpu.make_async_remote_copy(
        src_ref=edge.at[0],
        dst_ref=halo.at[1],
        send_sem=edge_send.at[0],
        recv_sem=edge_recv.at[1],
        device_id=(sky - 1, me),
        device_id_type=MESH,
    )
    to_high = pltpu.make_async_remote_copy(
        src_ref=edge.at[1],
        dst_ref=halo.at[0],
        send_sem=edge_send.at[1],
        recv_sem=edge_recv.at[0],
        device_id=(sky + 1, me),
        device_id_type=MESH,
    )

    @pl.when(has_low)
    def _():
        to_low.start()

    @pl.when(has_high)
    def _():
        to_high.start()

    for copy in copies:
        copy.wait_send()

    @pl.when(has_low)
    def _():
        to_low.wait_send()
        to_high.wait_recv()
        merged[0] += halo[0].astype(F32)

    @pl.when(has_high)
    def _():
        to_high.wait_send()
        to_low.wait_recv()
        merged[patches - 1] += halo[1].astype(F32)

    for row in range(BS * BS // LANES):
        span = slice(row * LANES, (row + 1) * LANES)
        out_ref[0, 0, :, span] = (sum_ref[0, 0, :, span] + merged[:, 0, row, :]) / (
            weight_ref[0, 0, :, span] + merged[:, 1, row, :]
        )


def shards(
    science,
    inverse_variance,
    template,
    filters,
    kernel_index,
    spatial_coeff,
    visit_offset,
    block_count,
    block_owner,
    block_slot,
    coadd_sum,
    coadd_weight,
    *,
    n,
    skies,
):
    visits, height, width = science.shape[2:]
    basis = filters.shape[0]
    patches = coadd_sum.shape[2]
    tiles = width // LANES
    strip = height * tiles // n
    patch_total = n * patches
    rows = BS * BS // LANES
    vmem = pl.BlockSpec(memory_space=pltpu.VMEM)
    smem = pl.BlockSpec(memory_space=pltpu.SMEM)
    dma = pltpu.SemaphoreType.DMA
    limit = 40 * 1024 * 1024
    strips = pl.pallas_call(
        functools.partial(align_kernel, n, visits),
        out_shape=jax.ShapeDtypeStruct((n, visits, strip, LANES), BF16),
        in_specs=[smem, vmem],
        out_specs=vmem,
        scratch_shapes=[
            pltpu.VMEM((n * strip, LANES), BF16),
            pltpu.VMEM((n, strip, LANES), BF16),
            pltpu.VMEM((n - 1, visits, strip, LANES), BF16),
            dma((n - 1,)),
            dma((n - 1,)),
            dma((n - 1,)),
            dma((n - 1,)),
        ],
        compiler_params=pltpu.CompilerParams(
            collective_id=0, has_side_effects=True, vmem_limit_bytes=limit
        ),
        name="align",
    )(visit_offset, template)
    difference, pay = pl.pallas_call(
        functools.partial(match_kernel, patch_total, patches),
        out_shape=(
            jax.ShapeDtypeStruct(science.shape, F32),
            jax.ShapeDtypeStruct((patch_total, 2, rows, LANES), BF16),
        ),
        in_specs=[vmem] * 6 + [smem] * 3,
        out_specs=(vmem, vmem),
        scratch_shapes=[
            pltpu.VMEM((visits, basis * height, width), BF16),
            pltpu.VMEM((3 * LANES, basis * LANES), BF16),
            pltpu.VMEM((visits, 2 * height, basis * LANES), BF16),
            pltpu.VMEM((visits, 2 * height, basis * LANES), BF16),
            pltpu.VMEM((2, tiles, height, LANES), F32),
            pltpu.VMEM((patch_total + 1, 2, rows, LANES), F32),
        ],
        compiler_params=pltpu.CompilerParams(vmem_limit_bytes=limit),
        name="match",
    )(
        strips,
        filters,
        kernel_index,
        spatial_coeff,
        science,
        inverse_variance,
        block_count,
        block_owner,
        block_slot,
    )
    coadd = pl.pallas_call(
        functools.partial(merge_kernel, n, skies, patches),
        out_shape=jax.ShapeDtypeStruct(coadd_sum.shape, F32),
        in_specs=[vmem] * 3,
        out_specs=vmem,
        scratch_shapes=[
            pltpu.VMEM((n - 1, patches, 2, rows, LANES), BF16),
            pltpu.VMEM((patches, 2, rows, LANES), F32),
            pltpu.VMEM((2, 2, rows, LANES), BF16),
            pltpu.VMEM((2, 2, rows, LANES), BF16),
            dma((n - 1,)),
            dma((n - 1,)),
            dma((2,)),
            dma((2,)),
        ],
        compiler_params=pltpu.CompilerParams(
            collective_id=1, has_side_effects=True, vmem_limit_bytes=limit
        ),
        name="merge",
    )(pay, coadd_sum, coadd_weight)
    return difference, coadd


def solution(mesh):
    return jax.shard_map(
        functools.partial(shards, n=mesh.shape["tile"], skies=mesh.shape["sky"]),
        mesh=mesh,
        in_specs=(
            P("sky", "tile", None, None, None),
            P("sky", "tile", None, None, None),
            P("sky", "tile", None, None),
            P(),
            P(),
            P("sky", "tile", None, None, None),
            P("sky", None),
            P("sky", "tile", None),
            P("sky", "tile", None),
            P("sky", "tile", None),
            P("sky", "tile", None, None),
            P("sky", "tile", None, None),
        ),
        out_specs=(P("sky", "tile", None, None, None), P("sky", "tile", None, None)),
        check_vma=False,
    )
```

```python
import functools

import jax
import jax.numpy as jnp
from jax import lax
from jax.experimental import pallas as pl
from jax.experimental.pallas import tpu as pltpu
from jax.sharding import PartitionSpec as P

BS = 64
LANES = 128
MESH = pl.DeviceIdType.MESH
F32 = jnp.float32
BF16 = jnp.bfloat16


def greet(peers):
    barrier = pltpu.get_barrier_semaphore()
    for peer in peers:
        pl.semaphore_signal(barrier, inc=1, device_id=peer, device_id_type=MESH)
    return barrier


def align_kernel(n, visits, offset_ref, template_ref, out_ref, own, held, outgoing, send1, recv1, send2, recv2):
    sky = lax.axis_index("sky")
    me = lax.axis_index("tile")
    peers = [lax.rem(me + k, n) for k in range(1, n)]
    barrier = greet([(sky, peer) for peer in peers])
    height, width = template_ref.shape[-2:]
    tiles = width // LANES
    strip = height * tiles // n
    for t in range(tiles):
        own[t * height : (t + 1) * height, :] = template_ref[0, 0, :, t * LANES : (t + 1) * LANES]
    pl.semaphore_wait(barrier, n - 1)
    first = []
    for k, peer in enumerate(peers):
        copy = pltpu.make_async_remote_copy(
            src_ref=own.at[pl.ds(pl.multiple_of(peer * strip, strip), strip)],
            dst_ref=held.at[me],
            send_sem=send1.at[k],
            recv_sem=recv1.at[k],
            device_id=(sky, peer),
            device_id_type=MESH,
        )
        copy.start()
        first.append(copy)
    held[me] = own[pl.ds(pl.multiple_of(me * strip, strip), strip), :]
    for copy in first:
        copy.wait_recv()
    second = []
    for k, peer in enumerate(peers):
        for v in range(visits):
            place = peer + offset_ref[0, v]
            place = jnp.where(place >= n, place - n, place)
            outgoing[k, v] = held[place]
        copy = pltpu.make_async_remote_copy(
            src_ref=outgoing.at[k],
            dst_ref=out_ref.at[me],
            send_sem=send2.at[k],
            recv_sem=recv2.at[k],
            device_id=(sky, peer),
            device_id_type=MESH,
        )
        copy.start()
        second.append(copy)
    for v in range(visits):
        place = me + offset_ref[0, v]
        place = jnp.where(place >= n, place - n, place)
        out_ref[me, v] = held[place]
    for copy in first:
        copy.wait_send()
    for copy in second:
        copy.wait()


def toeplitz(rows):
    return pltpu.roll(rows, 0, 1, stride=1, stride_axis=0)


def match_kernel(
    patch_total,
    patches,
    strips_ref,
    filters_ref,
    index_ref,
    coeff_ref,
    science_hbm,
    inverse_hbm,
    count_ref,
    owner_ref,
    slot_ref,
    diff_ref,
    pay_ref,
    filtered,
    row_band,
    band_high,
    band_low,
    image,
    total,
    science_ref,
    inverse_ref,
    arrived,
):
    fetches = [
        pltpu.make_async_copy(science_hbm, science_ref, arrived.at[0]),
        pltpu.make_async_copy(inverse_hbm, inverse_ref, arrived.at[1]),
    ]
    for fetch in fetches:
        fetch.start()
    n, visits, strip, lanes = strips_ref.shape
    height, width = science_ref.shape[-2:]
    tiles = width // LANES
    basis, taps = filters_ref.shape
    half = taps // 2
    kernels = index_ref.shape[0]

    tap_id = lax.broadcasted_iota(jnp.int32, (taps, LANES), 0)
    lane_id = lax.broadcasted_iota(jnp.int32, (taps, LANES), 1)
    spread_row = (lane_id == lax.rem(half - tap_id + LANES, LANES)).astype(BF16)
    spread_col = (lane_id == lax.rem(tap_id - half + LANES, LANES)).astype(BF16)
    filters = filters_ref[...]
    row_taps = jnp.dot(filters, spread_row, preferred_element_type=F32)
    col_taps = jnp.dot(filters, spread_col, preferred_element_type=F32).astype(BF16)

    y = lax.broadcasted_iota(jnp.int32, (height, LANES), 0)
    x = lax.broadcasted_iota(jnp.int32, (height, LANES), 1)
    gap = y - x
    near = jnp.abs(gap) <= half
    before = gap >= LANES - half
    after = gap <= half - LANES
    for j in range(basis):
        full = toeplitz(jnp.broadcast_to(row_taps[j : j + 1, :], (LANES, LANES)))
        span = slice(j * LANES, (j + 1) * LANES)
        row_band[0:LANES, span] = jnp.where(before, full, 0.0).astype(BF16)
        row_band[LANES : 2 * LANES, span] = jnp.where(near, full, 0.0).astype(BF16)
        row_band[2 * LANES : 3 * LANES, span] = jnp.where(after, full, 0.0).astype(BF16)

    index = index_ref[...]
    basis_id = lax.broadcasted_iota(jnp.int32, (kernels, basis), 1)
    pick_col = (index[:, 1:2] == basis_id).astype(BF16)
    kernel_taps = jnp.dot(pick_col, col_taps, preferred_element_type=F32)
    spread = jnp.concatenate(
        [jnp.where(index[:, 0:1] == j, kernel_taps, 0.0) for j in range(basis)], axis=1
    )
    downward = (2.0 * y.astype(F32) + (1.0 - height)) / height
    for v in range(visits):
        mixed = jnp.dot(
            coeff_ref[0, 0, v], spread, precision=lax.Precision.HIGHEST, preferred_element_type=F32
        )
        for j in range(basis):
            span = slice(j * LANES, (j + 1) * LANES)
            steady = mixed[0:1, span] + downward * mixed[2:3, span]
            across = jnp.broadcast_to(mixed[1:2, span], (height, LANES))
            for part, rows in enumerate((steady, across)):
                band = jnp.where(near, toeplitz(rows), 0.0)
                high = band.astype(BF16)
                down = slice(part * height, (part + 1) * height)
                band_high[v, down, span] = high
                band_low[v, down, span] = (band - high.astype(F32)).astype(BF16)

    per_tile = height // strip if strip <= height else 1
    source = []
    for t in range(tiles):
        rows = []
        for v in range(visits):
            rows += [strips_ref[t * per_tile + s, v] for s in range(per_tile)]
        source.append(jnp.concatenate(rows, axis=0))
    for t in range(tiles):
        low, top = max(t - 1, 0), min(t + 2, tiles)
        window = jnp.concatenate(source[low:top], axis=1)
        band = row_band[(low - t + 1) * LANES : (top - t + 1) * LANES, :]
        out = jnp.dot(window, band, preferred_element_type=F32).astype(BF16)
        for v in range(visits):
            for j in range(basis):
                filtered[v, j * height : (j + 1) * height, t * LANES : (t + 1) * LANES] = out[
                    v * height : (v + 1) * height, j * LANES : (j + 1) * LANES
                ]

    total[...] = jnp.zeros_like(total)
    for fetch in fetches:
        fetch.wait()
    x_id = lax.broadcasted_iota(jnp.int32, (1, width), 1).astype(F32)
    rightward = (2.0 * x_id + (1.0 - width)) / width
    low_lanes = lax.broadcasted_iota(jnp.int32, (BS // 2, LANES), 1) < BS
    downs = height // BS
    blocks = downs * (width // BS)
    for v in range(visits):
        operand = filtered[v]
        product = jnp.dot(band_high[v], operand, preferred_element_type=F32) + jnp.dot(
            band_low[v], operand, preferred_element_type=F32
        )
        difference = science_ref[0, 0, v] - (product[:height] + rightward * product[height:])
        diff_ref[0, 0, v] = difference
        inverse = inverse_ref[0, 0, v].astype(F32)
        weighted = inverse * difference
        for t in range(tiles):
            image[0, t] = weighted[:, t * LANES : (t + 1) * LANES]
            image[1, t] = inverse[:, t * LANES : (t + 1) * LANES]
        limit = count_ref[0, 0, v]
        for by in range(downs):
            for t in range(tiles):
                pair = []
                for side in range(2):
                    r = by * (width // BS) + 2 * t + side
                    spot = owner_ref[0, 0, v * blocks + r] * patches + slot_ref[0, 0, v * blocks + r]
                    pair.append(jnp.where(r < limit, spot, patch_total))
                for m in range(2):
                    even = image[m, t, pl.ds(by * BS, BS // 2, stride=2), :]
                    odd = image[m, t, pl.ds(by * BS + 1, BS // 2, stride=2), :]
                    left = jnp.where(low_lanes, even, pltpu.roll(odd, BS, 1))
                    right = jnp.where(low_lanes, pltpu.roll(even, BS, 1), odd)
                    total[pair[0], m] += left
                    total[pair[1], m] += right
    pay_ref[...] = total[0:patch_total].astype(BF16)


def merge_kernel(
    n, skies, patches, pay_ref, sum_ref, weight_ref, out_ref, landed, merged, edge, halo, send, recv, edge_send, edge_recv
):
    sky = lax.axis_index("sky")
    me = lax.axis_index("tile")
    peers = [lax.rem(me + k, n) for k in range(1, n)]
    barrier = greet([(sky, peer) for peer in peers])
    has_low = sky > 0
    has_high = sky < skies - 1

    @pl.when(has_low)
    def _():
        pl.semaphore_signal(barrier, inc=1, device_id=(sky - 1, me), device_id_type=MESH)

    @pl.when(has_high)
    def _():
        pl.semaphore_signal(barrier, inc=1, device_id=(sky + 1, me), device_id_type=MESH)

    around = jnp.where(has_low, 1, 0) + jnp.where(has_high, 1, 0)
    pl.semaphore_wait(barrier, n - 1 + around)
    copies = []
    for k, peer in enumerate(peers):
        copy = pltpu.make_async_remote_copy(
            src_ref=pay_ref.at[pl.ds(peer * patches, patches)],
            dst_ref=landed.at[k],
            send_sem=send.at[k],
            recv_sem=recv.at[k],
            device_id=(sky, peer),
            device_id_type=MESH,
        )
        copy.start()
        copies.append(copy)
    summed = pay_ref[pl.ds(me * patches, patches)].astype(F32)
    for k, copy in enumerate(copies):
        copy.wait_recv()
        summed = summed + landed[k].astype(F32)
    merged[...] = summed
    edge[0] = summed[0].astype(BF16)
    edge[1] = summed[patches - 1].astype(BF16)
    to_low = pltpu.make_async_remote_copy(
        src_ref=edge.at[0],
        dst_ref=halo.at[1],
        send_sem=edge_send.at[0],
        recv_sem=edge_recv.at[1],
        device_id=(sky - 1, me),
        device_id_type=MESH,
    )
    to_high = pltpu.make_async_remote_copy(
        src_ref=edge.at[1],
        dst_ref=halo.at[0],
        send_sem=edge_send.at[1],
        recv_sem=edge_recv.at[0],
        device_id=(sky + 1, me),
        device_id_type=MESH,
    )

    @pl.when(has_low)
    def _():
        to_low.start()

    @pl.when(has_high)
    def _():
        to_high.start()

    for copy in copies:
        copy.wait_send()

    @pl.when(has_low)
    def _():
        to_low.wait_send()
        to_high.wait_recv()
        merged[0] += halo[0].astype(F32)

    @pl.when(has_high)
    def _():
        to_high.wait_send()
        to_low.wait_recv()
        merged[patches - 1] += halo[1].astype(F32)

    for row in range(BS * BS // LANES):
        span = slice(row * LANES, (row + 1) * LANES)
        out_ref[0, 0, :, span] = (sum_ref[0, 0, :, span] + merged[:, 0, row, :]) / (
            weight_ref[0, 0, :, span] + merged[:, 1, row, :]
        )


def shards(
    science,
    inverse_variance,
    template,
    filters,
    kernel_index,
    spatial_coeff,
    visit_offset,
    block_count,
    block_owner,
    block_slot,
    coadd_sum,
    coadd_weight,
    *,
    n,
    skies,
):
    visits, height, width = science.shape[2:]
    basis = filters.shape[0]
    patches = coadd_sum.shape[2]
    tiles = width // LANES
    strip = height * tiles // n
    patch_total = n * patches
    rows = BS * BS // LANES
    vmem = pl.BlockSpec(memory_space=pltpu.VMEM)
    smem = pl.BlockSpec(memory_space=pltpu.SMEM)
    dma = pltpu.SemaphoreType.DMA
    limit = 40 * 1024 * 1024
    strips = pl.pallas_call(
        functools.partial(align_kernel, n, visits),
        out_shape=jax.ShapeDtypeStruct((n, visits, strip, LANES), BF16),
        in_specs=[smem, vmem],
        out_specs=vmem,
        scratch_shapes=[
            pltpu.VMEM((n * strip, LANES), BF16),
            pltpu.VMEM((n, strip, LANES), BF16),
            pltpu.VMEM((n - 1, visits, strip, LANES), BF16),
            dma((n - 1,)),
            dma((n - 1,)),
            dma((n - 1,)),
            dma((n - 1,)),
        ],
        compiler_params=pltpu.CompilerParams(
            collective_id=0, has_side_effects=True, vmem_limit_bytes=limit
        ),
        name="align",
    )(visit_offset, template)
    difference, pay = pl.pallas_call(
        functools.partial(match_kernel, patch_total, patches),
        out_shape=(
            jax.ShapeDtypeStruct(science.shape, F32),
            jax.ShapeDtypeStruct((patch_total, 2, rows, LANES), BF16),
        ),
        in_specs=[vmem] * 4 + [pl.BlockSpec(memory_space=pl.ANY)] * 2 + [smem] * 3,
        out_specs=(vmem, vmem),
        scratch_shapes=[
            pltpu.VMEM((visits, basis * height, width), BF16),
            pltpu.VMEM((3 * LANES, basis * LANES), BF16),
            pltpu.VMEM((visits, 2 * height, basis * LANES), BF16),
            pltpu.VMEM((visits, 2 * height, basis * LANES), BF16),
            pltpu.VMEM((2, tiles, height, LANES), F32),
            pltpu.VMEM((patch_total + 1, 2, rows, LANES), F32),
            pltpu.VMEM(science.shape, F32),
            pltpu.VMEM(inverse_variance.shape, BF16),
            dma((2,)),
        ],
        compiler_params=pltpu.CompilerParams(vmem_limit_bytes=limit),
        name="match",
    )(
        strips,
        filters,
        kernel_index,
        spatial_coeff,
        science,
        inverse_variance,
        block_count,
        block_owner,
        block_slot,
    )
    coadd = pl.pallas_call(
        functools.partial(merge_kernel, n, skies, patches),
        out_shape=jax.ShapeDtypeStruct(coadd_sum.shape, F32),
        in_specs=[vmem] * 3,
        out_specs=vmem,
        scratch_shapes=[
            pltpu.VMEM((n - 1, patches, 2, rows, LANES), BF16),
            pltpu.VMEM((patches, 2, rows, LANES), F32),
            pltpu.VMEM((2, 2, rows, LANES), BF16),
            pltpu.VMEM((2, 2, rows, LANES), BF16),
            dma((n - 1,)),
            dma((n - 1,)),
            dma((2,)),
            dma((2,)),
        ],
        compiler_params=pltpu.CompilerParams(
            collective_id=1, has_side_effects=True, vmem_limit_bytes=limit
        ),
        name="merge",
    )(pay, coadd_sum, coadd_weight)
    return difference, coadd


def solution(mesh):
    return jax.shard_map(
        functools.partial(shards, n=mesh.shape["tile"], skies=mesh.shape["sky"]),
        mesh=mesh,
        in_specs=(
            P("sky", "tile", None, None, None),
            P("sky", "tile", None, None, None),
            P("sky", "tile", None, None),
            P(),
            P(),
            P("sky", "tile", None, None, None),
            P("sky", None),
            P("sky", "tile", None),
            P("sky", "tile", None),
            P("sky", "tile", None),
            P("sky", "tile", None, None),
            P("sky", "tile", None, None),
        ),
        out_specs=(P("sky", "tile", None, None, None), P("sky", "tile", None, None)),
        check_vma=False,
    )
```

```python
import functools

import jax
import jax.numpy as jnp
from jax import lax
from jax.experimental import pallas as pl
from jax.experimental.pallas import tpu as pltpu
from jax.sharding import PartitionSpec as P

BS = 64
LANES = 128
MESH = pl.DeviceIdType.MESH
F32 = jnp.float32
BF16 = jnp.bfloat16


def greet(peers):
    barrier = pltpu.get_barrier_semaphore()
    for peer in peers:
        pl.semaphore_signal(barrier, inc=1, device_id=peer, device_id_type=MESH)
    return barrier


def align_kernel(n, visits, offset_ref, template_ref, out_ref, own, held, outgoing, send1, recv1, send2, recv2):
    sky = lax.axis_index("sky")
    me = lax.axis_index("tile")
    peers = [lax.rem(me + k, n) for k in range(1, n)]
    barrier = greet([(sky, peer) for peer in peers])
    height, width = template_ref.shape[-2:]
    tiles = width // LANES
    strip = height * tiles // n
    for t in range(tiles):
        own[t * height : (t + 1) * height, :] = template_ref[0, 0, :, t * LANES : (t + 1) * LANES]
    pl.semaphore_wait(barrier, n - 1)
    first = []
    for k, peer in enumerate(peers):
        copy = pltpu.make_async_remote_copy(
            src_ref=own.at[pl.ds(pl.multiple_of(peer * strip, strip), strip)],
            dst_ref=held.at[me],
            send_sem=send1.at[k],
            recv_sem=recv1.at[k],
            device_id=(sky, peer),
            device_id_type=MESH,
        )
        copy.start()
        first.append(copy)
    held[me] = own[pl.ds(pl.multiple_of(me * strip, strip), strip), :]
    for copy in first:
        copy.wait_recv()
    second = []
    for k, peer in enumerate(peers):
        for v in range(visits):
            place = peer + offset_ref[0, v]
            place = jnp.where(place >= n, place - n, place)
            outgoing[k, v] = held[place]
        copy = pltpu.make_async_remote_copy(
            src_ref=outgoing.at[k],
            dst_ref=out_ref.at[me],
            send_sem=send2.at[k],
            recv_sem=recv2.at[k],
            device_id=(sky, peer),
            device_id_type=MESH,
        )
        copy.start()
        second.append(copy)
    for v in range(visits):
        place = me + offset_ref[0, v]
        place = jnp.where(place >= n, place - n, place)
        out_ref[me, v] = held[place]
    for copy in first:
        copy.wait_send()
    for copy in second:
        copy.wait()


def toeplitz(rows):
    return pltpu.roll(rows, 0, 1, stride=1, stride_axis=0)


def match_kernel(
    patch_total,
    patches,
    strips_ref,
    filters_ref,
    index_ref,
    coeff_ref,
    science_hbm,
    inverse_hbm,
    count_ref,
    owner_ref,
    slot_ref,
    diff_ref,
    pay_ref,
    filtered,
    row_band,
    band_high,
    band_low,
    image,
    total,
    science_ref,
    inverse_ref,
    arrived,
):
    fetches = [
        pltpu.make_async_copy(science_hbm, science_ref, arrived.at[0]),
        pltpu.make_async_copy(inverse_hbm, inverse_ref, arrived.at[1]),
    ]
    for fetch in fetches:
        fetch.start()
    n, visits, strip, lanes = strips_ref.shape
    height, width = science_ref.shape[-2:]
    tiles = width // LANES
    basis, taps = filters_ref.shape
    half = taps // 2
    kernels = index_ref.shape[0]

    tap_id = lax.broadcasted_iota(jnp.int32, (taps, LANES), 0)
    lane_id = lax.broadcasted_iota(jnp.int32, (taps, LANES), 1)
    spread_row = (lane_id == lax.rem(half - tap_id + LANES, LANES)).astype(BF16)
    spread_col = (lane_id == lax.rem(tap_id - half + LANES, LANES)).astype(BF16)
    filters = filters_ref[...]
    row_taps = jnp.dot(filters, spread_row, preferred_element_type=F32)
    col_taps = jnp.dot(filters, spread_col, preferred_element_type=F32).astype(BF16)

    y = lax.broadcasted_iota(jnp.int32, (height, LANES), 0)
    x = lax.broadcasted_iota(jnp.int32, (height, LANES), 1)
    gap = y - x
    near = jnp.abs(gap) <= half
    before = gap >= LANES - half
    after = gap <= half - LANES
    for j in range(basis):
        full = toeplitz(jnp.broadcast_to(row_taps[j : j + 1, :], (LANES, LANES)))
        span = slice(j * LANES, (j + 1) * LANES)
        row_band[0:LANES, span] = jnp.where(before, full, 0.0).astype(BF16)
        row_band[LANES : 2 * LANES, span] = jnp.where(near, full, 0.0).astype(BF16)
        row_band[2 * LANES : 3 * LANES, span] = jnp.where(after, full, 0.0).astype(BF16)

    index = index_ref[...]
    basis_id = lax.broadcasted_iota(jnp.int32, (kernels, basis), 1)
    pick_col = (index[:, 1:2] == basis_id).astype(BF16)
    kernel_taps = jnp.dot(pick_col, col_taps, preferred_element_type=F32)
    spread = jnp.concatenate(
        [jnp.where(index[:, 0:1] == j, kernel_taps, 0.0) for j in range(basis)], axis=1
    )
    downward = (2.0 * y.astype(F32) + (1.0 - height)) / height
    for v in range(visits):
        mixed = jnp.dot(
            coeff_ref[0, 0, v], spread, precision=lax.Precision.HIGHEST, preferred_element_type=F32
        )
        for j in range(basis):
            span = slice(j * LANES, (j + 1) * LANES)
            steady = mixed[0:1, span] + downward * mixed[2:3, span]
            across = jnp.broadcast_to(mixed[1:2, span], (height, LANES))
            for part, rows in enumerate((steady, across)):
                band = jnp.where(near, toeplitz(rows), 0.0)
                high = band.astype(BF16)
                down = slice(part * height, (part + 1) * height)
                band_high[v, down, span] = high
                band_low[v, down, span] = (band - high.astype(F32)).astype(BF16)

    per_tile = height // strip if strip <= height else 1
    source = []
    for t in range(tiles):
        rows = []
        for v in range(visits):
            rows += [strips_ref[t * per_tile + s, v] for s in range(per_tile)]
        source.append(jnp.concatenate(rows, axis=0))
    for t in range(tiles):
        low, top = max(t - 1, 0), min(t + 2, tiles)
        window = jnp.concatenate(source[low:top], axis=1)
        band = row_band[(low - t + 1) * LANES : (top - t + 1) * LANES, :]
        out = jnp.dot(window, band, preferred_element_type=F32).astype(BF16)
        for v in range(visits):
            for j in range(basis):
                filtered[v, j * height : (j + 1) * height, t * LANES : (t + 1) * LANES] = out[
                    v * height : (v + 1) * height, j * LANES : (j + 1) * LANES
                ]

    total[...] = jnp.zeros_like(total)
    for fetch in fetches:
        fetch.wait()
    x_id = lax.broadcasted_iota(jnp.int32, (1, width), 1).astype(F32)
    rightward = (2.0 * x_id + (1.0 - width)) / width
    low_lanes = lax.broadcasted_iota(jnp.int32, (BS // 2, LANES), 1) < BS
    downs = height // BS
    blocks = downs * (width // BS)
    for v in range(visits):
        operand = filtered[v]
        product = jnp.dot(band_high[v], operand, preferred_element_type=F32) + jnp.dot(
            band_low[v], operand, preferred_element_type=F32
        )
        difference = science_ref[0, 0, v] - (product[:height] + rightward * product[height:])
        diff_ref[0, 0, v] = difference
        inverse = inverse_ref[0, 0, v].astype(F32)
        weighted = inverse * difference
        for t in range(tiles):
            image[0, t] = weighted[:, t * LANES : (t + 1) * LANES]
            image[1, t] = inverse[:, t * LANES : (t + 1) * LANES]
        limit = count_ref[0, 0, v]
        for by in range(downs):
            for t in range(tiles):
                pair = []
                for side in range(2):
                    r = by * (width // BS) + 2 * t + side
                    spot = owner_ref[0, 0, v * blocks + r] * patches + slot_ref[0, 0, v * blocks + r]
                    pair.append(jnp.where(r < limit, spot, patch_total))
                for m in range(2):
                    even = image[m, t, pl.ds(by * BS, BS // 2, stride=2), :]
                    odd = image[m, t, pl.ds(by * BS + 1, BS // 2, stride=2), :]
                    left = jnp.where(low_lanes, even, pltpu.roll(odd, BS, 1))
                    right = jnp.where(low_lanes, pltpu.roll(even, BS, 1), odd)
                    total[pair[0], m] += left
                    total[pair[1], m] += right
    pay_ref[...] = total[0:patch_total].astype(BF16)


def merge_kernel(
    n, skies, patches, pay_ref, sum_ref, weight_ref, out_ref, landed, merged, edge, halo, send, recv, edge_send, edge_recv
):
    sky = lax.axis_index("sky")
    me = lax.axis_index("tile")
    peers = [lax.rem(me + k, n) for k in range(1, n)]
    barrier = greet([(sky, peer) for peer in peers])
    has_low = sky > 0
    has_high = sky < skies - 1

    @pl.when(has_low)
    def _():
        pl.semaphore_signal(barrier, inc=1, device_id=(sky - 1, me), device_id_type=MESH)

    @pl.when(has_high)
    def _():
        pl.semaphore_signal(barrier, inc=1, device_id=(sky + 1, me), device_id_type=MESH)

    around = jnp.where(has_low, 1, 0) + jnp.where(has_high, 1, 0)
    pl.semaphore_wait(barrier, n - 1 + around)
    copies = []
    for k, peer in enumerate(peers):
        copy = pltpu.make_async_remote_copy(
            src_ref=pay_ref.at[pl.ds(peer * patches, patches)],
            dst_ref=landed.at[k],
            send_sem=send.at[k],
            recv_sem=recv.at[k],
            device_id=(sky, peer),
            device_id_type=MESH,
        )
        copy.start()
        copies.append(copy)
    summed = pay_ref[pl.ds(me * patches, patches)].astype(F32)
    for k, copy in enumerate(copies):
        copy.wait_recv()
        summed = summed + landed[k].astype(F32)
    merged[...] = summed
    edge[0] = summed[0].astype(BF16)
    edge[1] = summed[patches - 1].astype(BF16)
    to_low = pltpu.make_async_remote_copy(
        src_ref=edge.at[0],
        dst_ref=halo.at[1],
        send_sem=edge_send.at[0],
        recv_sem=edge_recv.at[1],
        device_id=(sky - 1, me),
        device_id_type=MESH,
    )
    to_high = pltpu.make_async_remote_copy(
        src_ref=edge.at[1],
        dst_ref=halo.at[0],
        send_sem=edge_send.at[1],
        recv_sem=edge_recv.at[0],
        device_id=(sky + 1, me),
        device_id_type=MESH,
    )

    @pl.when(has_low)
    def _():
        to_low.start()

    @pl.when(has_high)
    def _():
        to_high.start()

    for copy in copies:
        copy.wait_send()

    @pl.when(has_low)
    def _():
        to_low.wait_send()
        to_high.wait_recv()
        merged[0] += halo[0].astype(F32)

    @pl.when(has_high)
    def _():
        to_high.wait_send()
        to_low.wait_recv()
        merged[patches - 1] += halo[1].astype(F32)

    for row in range(BS * BS // LANES):
        span = slice(row * LANES, (row + 1) * LANES)
        out_ref[0, 0, :, span] = (sum_ref[0, 0, :, span] + merged[:, 0, row, :]) / (
            weight_ref[0, 0, :, span] + merged[:, 1, row, :]
        )


def shards(
    science,
    inverse_variance,
    template,
    filters,
    kernel_index,
    spatial_coeff,
    visit_offset,
    block_count,
    block_owner,
    block_slot,
    coadd_sum,
    coadd_weight,
    *,
    n,
    skies,
):
    visits, height, width = science.shape[2:]
    basis = filters.shape[0]
    patches = coadd_sum.shape[2]
    tiles = width // LANES
    strip = height * tiles // n
    patch_total = n * patches
    rows = BS * BS // LANES
    vmem = pl.BlockSpec(memory_space=pltpu.VMEM)
    smem = pl.BlockSpec(memory_space=pltpu.SMEM)
    dma = pltpu.SemaphoreType.DMA
    strips = pl.pallas_call(
        functools.partial(align_kernel, n, visits),
        out_shape=jax.ShapeDtypeStruct((n, visits, strip, LANES), BF16),
        in_specs=[smem, vmem],
        out_specs=vmem,
        scratch_shapes=[
            pltpu.VMEM((n * strip, LANES), BF16),
            pltpu.VMEM((n, strip, LANES), BF16),
            pltpu.VMEM((n - 1, visits, strip, LANES), BF16),
            dma((n - 1,)),
            dma((n - 1,)),
            dma((n - 1,)),
            dma((n - 1,)),
        ],
        compiler_params=pltpu.CompilerParams(
            collective_id=0, has_side_effects=True
        ),
        name="align",
    )(visit_offset, template)
    difference, pay = pl.pallas_call(
        functools.partial(match_kernel, patch_total, patches),
        out_shape=(
            jax.ShapeDtypeStruct(science.shape, F32),
            jax.ShapeDtypeStruct((patch_total, 2, rows, LANES), BF16),
        ),
        in_specs=[vmem] * 4 + [pl.BlockSpec(memory_space=pl.ANY)] * 2 + [smem] * 3,
        out_specs=(vmem, vmem),
        scratch_shapes=[
            pltpu.VMEM((visits, basis * height, width), BF16),
            pltpu.VMEM((3 * LANES, basis * LANES), BF16),
            pltpu.VMEM((visits, 2 * height, basis * LANES), BF16),
            pltpu.VMEM((visits, 2 * height, basis * LANES), BF16),
            pltpu.VMEM((2, tiles, height, LANES), F32),
            pltpu.VMEM((patch_total + 1, 2, rows, LANES), F32),
            pltpu.VMEM(science.shape, F32),
            pltpu.VMEM(inverse_variance.shape, BF16),
            dma((2,)),
        ],
        compiler_params=pltpu.CompilerParams(),
        name="match",
    )(
        strips,
        filters,
        kernel_index,
        spatial_coeff,
        science,
        inverse_variance,
        block_count,
        block_owner,
        block_slot,
    )
    coadd = pl.pallas_call(
        functools.partial(merge_kernel, n, skies, patches),
        out_shape=jax.ShapeDtypeStruct(coadd_sum.shape, F32),
        in_specs=[vmem] * 3,
        out_specs=vmem,
        scratch_shapes=[
            pltpu.VMEM((n - 1, patches, 2, rows, LANES), BF16),
            pltpu.VMEM((patches, 2, rows, LANES), F32),
            pltpu.VMEM((2, 2, rows, LANES), BF16),
            pltpu.VMEM((2, 2, rows, LANES), BF16),
            dma((n - 1,)),
            dma((n - 1,)),
            dma((2,)),
            dma((2,)),
        ],
        compiler_params=pltpu.CompilerParams(
            collective_id=1, has_side_effects=True
        ),
        name="merge",
    )(pay, coadd_sum, coadd_weight)
    return difference, coadd


def solution(mesh):
    return jax.shard_map(
        functools.partial(shards, n=mesh.shape["tile"], skies=mesh.shape["sky"]),
        mesh=mesh,
        in_specs=(
            P("sky", "tile", None, None, None),
            P("sky", "tile", None, None, None),
            P("sky", "tile", None, None),
            P(),
            P(),
            P("sky", "tile", None, None, None),
            P("sky", None),
            P("sky", "tile", None),
            P("sky", "tile", None),
            P("sky", "tile", None),
            P("sky", "tile", None, None),
            P("sky", "tile", None, None),
        ),
        out_specs=(P("sky", "tile", None, None, None), P("sky", "tile", None, None)),
        check_vma=False,
    )
```

```python
import functools

import jax
import jax.numpy as jnp
from jax import lax
from jax.experimental import pallas as pl
from jax.experimental.pallas import tpu as pltpu
from jax.sharding import PartitionSpec as P

BS = 64
LANES = 128
MESH = pl.DeviceIdType.MESH
F32 = jnp.float32
BF16 = jnp.bfloat16


def greet(peers):
    barrier = pltpu.get_barrier_semaphore()
    for peer in peers:
        pl.semaphore_signal(barrier, inc=1, device_id=peer, device_id_type=MESH)
    return barrier


def align_kernel(n, visits, offset_ref, template_ref, out_ref, own, held, outgoing, send1, recv1, send2, recv2):
    sky = lax.axis_index("sky")
    me = lax.axis_index("tile")
    peers = [lax.rem(me + k, n) for k in range(1, n)]
    barrier = greet([(sky, peer) for peer in peers])
    height, width = template_ref.shape[-2:]
    tiles = width // LANES
    strip = height * tiles // n
    for t in range(tiles):
        own[t * height : (t + 1) * height, :] = template_ref[0, 0, :, t * LANES : (t + 1) * LANES]
    pl.semaphore_wait(barrier, n - 1)
    first = []
    for k, peer in enumerate(peers):
        copy = pltpu.make_async_remote_copy(
            src_ref=own.at[pl.ds(pl.multiple_of(peer * strip, strip), strip)],
            dst_ref=held.at[me],
            send_sem=send1.at[k],
            recv_sem=recv1.at[k],
            device_id=(sky, peer),
            device_id_type=MESH,
        )
        copy.start()
        first.append(copy)
    held[me] = own[pl.ds(pl.multiple_of(me * strip, strip), strip), :]
    for copy in first:
        copy.wait_recv()
    second = []
    for k, peer in enumerate(peers):
        for v in range(visits):
            place = peer + offset_ref[0, v]
            place = jnp.where(place >= n, place - n, place)
            outgoing[k, v] = held[place]
        copy = pltpu.make_async_remote_copy(
            src_ref=outgoing.at[k],
            dst_ref=out_ref.at[me],
            send_sem=send2.at[k],
            recv_sem=recv2.at[k],
            device_id=(sky, peer),
            device_id_type=MESH,
        )
        copy.start()
        second.append(copy)
    for v in range(visits):
        place = me + offset_ref[0, v]
        place = jnp.where(place >= n, place - n, place)
        out_ref[me, v] = held[place]
    for copy in first:
        copy.wait_send()
    for copy in second:
        copy.wait()


def toeplitz(rows):
    return pltpu.roll(rows, 0, 1, stride=1, stride_axis=0)


def match_kernel(
    patch_total,
    patches,
    strips_ref,
    filters_ref,
    index_ref,
    coeff_ref,
    science_hbm,
    inverse_hbm,
    count_ref,
    owner_ref,
    slot_ref,
    diff_ref,
    pay_ref,
    filtered,
    row_band,
    band_high,
    band_low,
    image,
    total,
    science_ref,
    inverse_ref,
    arrived,
):
    fetches = [
        pltpu.make_async_copy(science_hbm, science_ref, arrived.at[0]),
        pltpu.make_async_copy(inverse_hbm, inverse_ref, arrived.at[1]),
    ]
    for fetch in fetches:
        fetch.start()
    n, visits, strip, lanes = strips_ref.shape
    height, width = science_ref.shape[-2:]
    tiles = width // LANES
    basis, taps = filters_ref.shape
    half = taps // 2
    kernels = index_ref.shape[0]

    tap_id = lax.broadcasted_iota(jnp.int32, (taps, LANES), 0)
    lane_id = lax.broadcasted_iota(jnp.int32, (taps, LANES), 1)
    spread_row = (lane_id == lax.rem(half - tap_id + LANES, LANES)).astype(BF16)
    spread_col = (lane_id == lax.rem(tap_id - half + LANES, LANES)).astype(BF16)
    filters = filters_ref[...]
    row_taps = jnp.dot(filters, spread_row, preferred_element_type=F32)
    col_taps = jnp.dot(filters, spread_col, preferred_element_type=F32).astype(BF16)

    y = lax.broadcasted_iota(jnp.int32, (height, LANES), 0)
    x = lax.broadcasted_iota(jnp.int32, (height, LANES), 1)
    gap = y - x
    near = jnp.abs(gap) <= half
    before = gap >= LANES - half
    after = gap <= half - LANES
    for j in range(basis):
        full = toeplitz(jnp.broadcast_to(row_taps[j : j + 1, :], (LANES, LANES)))
        span = slice(j * LANES, (j + 1) * LANES)
        row_band[0:LANES, span] = jnp.where(before, full, 0.0).astype(BF16)
        row_band[LANES : 2 * LANES, span] = jnp.where(near, full, 0.0).astype(BF16)
        row_band[2 * LANES : 3 * LANES, span] = jnp.where(after, full, 0.0).astype(BF16)

    index = index_ref[...]
    basis_id = lax.broadcasted_iota(jnp.int32, (kernels, basis), 1)
    pick_col = (index[:, 1:2] == basis_id).astype(BF16)
    kernel_taps = jnp.dot(pick_col, col_taps, preferred_element_type=F32)
    spread = jnp.concatenate(
        [jnp.where(index[:, 0:1] == j, kernel_taps, 0.0) for j in range(basis)], axis=1
    )
    downward = (2.0 * y.astype(F32) + (1.0 - height)) / height
    for v in range(visits):
        mixed = jnp.dot(
            coeff_ref[0, 0, v], spread, precision=lax.Precision.HIGHEST, preferred_element_type=F32
        )
        for j in range(basis):
            span = slice(j * LANES, (j + 1) * LANES)
            steady = mixed[0:1, span] + downward * mixed[2:3, span]
            across = jnp.broadcast_to(mixed[1:2, span], (height, LANES))
            for part, rows in enumerate((steady, across)):
                band = jnp.where(near, toeplitz(rows), 0.0)
                high = band.astype(BF16)
                down = slice(part * height, (part + 1) * height)
                band_high[v, down, span] = high
                band_low[v, down, span] = (band - high.astype(F32)).astype(BF16)

    per_tile = height // strip if strip <= height else 1
    source = []
    for t in range(tiles):
        rows = []
        for v in range(visits):
            rows += [strips_ref[t * per_tile + s, v] for s in range(per_tile)]
        source.append(jnp.concatenate(rows, axis=0))
    for t in range(tiles):
        low, top = max(t - 1, 0), min(t + 2, tiles)
        window = jnp.concatenate(source[low:top], axis=1)
        band = row_band[(low - t + 1) * LANES : (top - t + 1) * LANES, :]
        out = jnp.dot(window, band, preferred_element_type=F32).astype(BF16)
        for v in range(visits):
            for j in range(basis):
                filtered[v, j * height : (j + 1) * height, t * LANES : (t + 1) * LANES] = out[
                    v * height : (v + 1) * height, j * LANES : (j + 1) * LANES
                ]

    total[...] = jnp.zeros_like(total)
    for fetch in fetches:
        fetch.wait()
    x_id = lax.broadcasted_iota(jnp.int32, (1, width), 1).astype(F32)
    rightward = (2.0 * x_id + (1.0 - width)) / width
    low_lanes = lax.broadcasted_iota(jnp.int32, (BS // 2, LANES), 1) < BS
    downs = height // BS
    blocks = downs * (width // BS)
    for v in range(visits):
        operand = filtered[v]
        product = jnp.dot(band_high[v], operand, preferred_element_type=F32) + jnp.dot(
            band_low[v], operand, preferred_element_type=F32
        )
        difference = science_ref[0, 0, v] - (product[:height] + rightward * product[height:])
        diff_ref[0, 0, v] = difference
        inverse = inverse_ref[0, 0, v].astype(F32)
        weighted = inverse * difference
        for t in range(tiles):
            image[0, t] = weighted[:, t * LANES : (t + 1) * LANES]
            image[1, t] = inverse[:, t * LANES : (t + 1) * LANES]
        limit = count_ref[0, 0, v]
        for by in range(downs):
            for t in range(tiles):
                pair = []
                for side in range(2):
                    r = by * (width // BS) + 2 * t + side
                    spot = owner_ref[0, 0, v * blocks + r] * patches + slot_ref[0, 0, v * blocks + r]
                    pair.append(jnp.where(r < limit, spot, patch_total))
                for m in range(2):
                    even = image[m, t, pl.ds(by * BS, BS // 2, stride=2), :]
                    odd = image[m, t, pl.ds(by * BS + 1, BS // 2, stride=2), :]
                    left = jnp.where(low_lanes, even, pltpu.roll(odd, BS, 1))
                    right = jnp.where(low_lanes, pltpu.roll(even, BS, 1), odd)
                    total[pair[0], m] += left
                    total[pair[1], m] += right
    pay_ref[...] = total[0:patch_total].astype(BF16)


def merge_kernel(
    n, skies, patches, pay_ref, sum_ref, weight_ref, out_ref, landed, merged, edge, halo, send, recv, edge_send, edge_recv
):
    sky = lax.axis_index("sky")
    me = lax.axis_index("tile")
    peers = [lax.rem(me + k, n) for k in range(1, n)]
    barrier = greet([(sky, peer) for peer in peers])
    has_low = sky > 0
    has_high = sky < skies - 1

    @pl.when(has_low)
    def _():
        pl.semaphore_signal(barrier, inc=1, device_id=(sky - 1, me), device_id_type=MESH)

    @pl.when(has_high)
    def _():
        pl.semaphore_signal(barrier, inc=1, device_id=(sky + 1, me), device_id_type=MESH)

    around = jnp.where(has_low, 1, 0) + jnp.where(has_high, 1, 0)
    pl.semaphore_wait(barrier, n - 1 + around)
    copies = []
    for k, peer in enumerate(peers):
        copy = pltpu.make_async_remote_copy(
            src_ref=pay_ref.at[pl.ds(peer * patches, patches)],
            dst_ref=landed.at[k],
            send_sem=send.at[k],
            recv_sem=recv.at[k],
            device_id=(sky, peer),
            device_id_type=MESH,
        )
        copy.start()
        copies.append(copy)
    summed = pay_ref[pl.ds(me * patches, patches)].astype(F32)
    for k, copy in enumerate(copies):
        copy.wait_recv()
        summed = summed + landed[k].astype(F32)
    merged[...] = summed
    edge[0] = summed[0].astype(BF16)
    edge[1] = summed[patches - 1].astype(BF16)
    to_low = pltpu.make_async_remote_copy(
        src_ref=edge.at[0],
        dst_ref=halo.at[1],
        send_sem=edge_send.at[0],
        recv_sem=edge_recv.at[1],
        device_id=(sky - 1, me),
        device_id_type=MESH,
    )
    to_high = pltpu.make_async_remote_copy(
        src_ref=edge.at[1],
        dst_ref=halo.at[0],
        send_sem=edge_send.at[1],
        recv_sem=edge_recv.at[0],
        device_id=(sky + 1, me),
        device_id_type=MESH,
    )

    @pl.when(has_low)
    def _():
        to_low.start()

    @pl.when(has_high)
    def _():
        to_high.start()

    for copy in copies:
        copy.wait_send()

    @pl.when(has_low)
    def _():
        to_low.wait_send()
        to_high.wait_recv()
        merged[0] += halo[0].astype(F32)

    @pl.when(has_high)
    def _():
        to_high.wait_send()
        to_low.wait_recv()
        merged[patches - 1] += halo[1].astype(F32)

    for row in range(BS * BS // LANES):
        span = slice(row * LANES, (row + 1) * LANES)
        out_ref[0, 0, :, span] = (sum_ref[0, 0, :, span] + merged[:, 0, row, :]) / (
            weight_ref[0, 0, :, span] + merged[:, 1, row, :]
        )


def shards(
    science,
    inverse_variance,
    template,
    filters,
    kernel_index,
    spatial_coeff,
    visit_offset,
    block_count,
    block_owner,
    block_slot,
    coadd_sum,
    coadd_weight,
    *,
    n,
    skies,
):
    visits, height, width = science.shape[2:]
    basis = filters.shape[0]
    patches = coadd_sum.shape[2]
    tiles = width // LANES
    strip = height * tiles // n
    patch_total = n * patches
    rows = BS * BS // LANES
    vmem = pl.BlockSpec(memory_space=pltpu.VMEM)
    smem = pl.BlockSpec(memory_space=pltpu.SMEM)
    dma = pltpu.SemaphoreType.DMA
    strips = pl.pallas_call(
        functools.partial(align_kernel, n, visits),
        out_shape=jax.ShapeDtypeStruct((n, visits, strip, LANES), BF16),
        in_specs=[smem, vmem],
        out_specs=vmem,
        scratch_shapes=[
            pltpu.VMEM((n * strip, LANES), BF16),
            pltpu.VMEM((n, strip, LANES), BF16),
            pltpu.VMEM((n - 1, visits, strip, LANES), BF16),
            dma((n - 1,)),
            dma((n - 1,)),
            dma((n - 1,)),
            dma((n - 1,)),
        ],
        compiler_params=pltpu.CompilerParams(
            collective_id=0, has_side_effects=True
        ),
        name="align",
    )(visit_offset, template)
    difference, pay = pl.pallas_call(
        functools.partial(match_kernel, patch_total, patches),
        out_shape=(
            jax.ShapeDtypeStruct(science.shape, F32),
            jax.ShapeDtypeStruct((patch_total, 2, rows, LANES), BF16),
        ),
        in_specs=[vmem] * 4 + [pl.BlockSpec(memory_space=pl.ANY)] * 2 + [smem] * 3,
        out_specs=(vmem, vmem),
        scratch_shapes=[
            pltpu.VMEM((visits, basis * height, width), BF16),
            pltpu.VMEM((3 * LANES, basis * LANES), BF16),
            pltpu.VMEM((visits, 2 * height, basis * LANES), BF16),
            pltpu.VMEM((visits, 2 * height, basis * LANES), BF16),
            pltpu.VMEM((2, tiles, height, LANES), F32),
            pltpu.VMEM((patch_total + 1, 2, rows, LANES), F32),
            pltpu.VMEM(science.shape, F32),
            pltpu.VMEM(inverse_variance.shape, BF16),
            dma((2,)),
        ],
        compiler_params=pltpu.CompilerParams(),
        name="match",
    )(
        strips,
        filters,
        kernel_index,
        spatial_coeff,
        science,
        inverse_variance,
        block_count,
        block_owner,
        block_slot,
    )
    coadd = pl.pallas_call(
        functools.partial(merge_kernel, n, skies, patches),
        out_shape=jax.ShapeDtypeStruct(coadd_sum.shape, F32),
        in_specs=[vmem] * 3,
        out_specs=vmem,
        scratch_shapes=[
            pltpu.VMEM((n - 1, patches, 2, rows, LANES), BF16),
            pltpu.VMEM((patches, 2, rows, LANES), F32),
            pltpu.VMEM((2, 2, rows, LANES), BF16),
            pltpu.VMEM((2, 2, rows, LANES), BF16),
            dma((n - 1,)),
            dma((n - 1,)),
            dma((2,)),
            dma((2,)),
        ],
        compiler_params=pltpu.CompilerParams(
            collective_id=1, has_side_effects=True, vmem_limit_bytes=40 * 1024 * 1024
        ),
        name="merge",
    )(pay, coadd_sum, coadd_weight)
    return difference, coadd


def solution(mesh):
    return jax.shard_map(
        functools.partial(shards, n=mesh.shape["tile"], skies=mesh.shape["sky"]),
        mesh=mesh,
        in_specs=(
            P("sky", "tile", None, None, None),
            P("sky", "tile", None, None, None),
            P("sky", "tile", None, None),
            P(),
            P(),
            P("sky", "tile", None, None, None),
            P("sky", None),
            P("sky", "tile", None),
            P("sky", "tile", None),
            P("sky", "tile", None),
            P("sky", "tile", None, None),
            P("sky", "tile", None, None),
        ),
        out_specs=(P("sky", "tile", None, None, None), P("sky", "tile", None, None)),
        check_vma=False,
    )
```
